32 devices in a mesh: frame: 4 (over x, core), fsdp: 8 (over z, y).
Axes of the slice: x: 2, y: 2, z: 4, core: 2. Of those that a mesh axis runs over, the one named last changes fastest.
Arguments:
- window: bfloat16 [4, 128, 5120], P('frame', 'fsdp'), may hold values from -6 to 6
- levels: int32 [4], P('frame'), may hold values from 0 to 15
- actions: int32 [4], P('frame'), may hold values from 0 to 15
- cache_len: int32 [1], replicated, may hold values from 128 to 1920
- level_table: float32 [16, 3, 5120], replicated, may hold values from -4 to 4
- action_table: float32 [16, 3, 5120], replicated, may hold values from -4 to 4
- w_qkv: bfloat16 [3, 5120, 4096], P(None, None, 'fsdp'), may hold values from -0.078125 to 0.078125
- w_out: bfloat16 [4096, 5120], P('fsdp'), may hold values from -0.09375 to 0.09375
- cache_keys: bfloat16 [2048, 4096], P('frame', 'fsdp'), may hold values from -220 to 220
- cache_values: bfloat16 [2048, 4096], P('frame', 'fsdp'), may hold values from -6 to 6
- fresh_frame: bfloat16 [128, 5120], P('fsdp'), may hold values from -6 to 6
Outputs:
- next_window: bfloat16 [4, 128, 5120], P('frame', 'fsdp')
- finished: bfloat16 [128, 5120], P('fsdp')
- new_cache_keys: bfloat16 [2048, 4096], P('frame', 'fsdp')
- new_cache_values: bfloat16 [2048, 4096], P('frame', 'fsdp')
The draws below stay inside these ranges and needn't reach their ends.
Inputs may be any that keep to these rules, and one draw needn't show every extreme that they name: Rows of the cache from cache_len on are unused.
All inputs are finite; a program needn't handle non-finite values.
Results may differ from the reference program's by a relative error of at most 0.015.
The reference program's roundings to bfloat16 on the way (of `normed`, `attended` and `updated`) count: a program that leaves them out, or rounds other values in their place, can miss the bound.
Values may be sent and summed in bfloat16 or wider, within the bound.
A program may use at most 128 MiB of HBM per device.

```python
import math
import jax
import jax.numpy as jnp
from jax import lax

D = 5120
H = 32
HD = 128
LEVELS = 16
ACTIONS = 16
WINDOW = 4
FT = 128
CACHE = 2048


def draw_cache_keys(key, part):
    shape = (CACHE, H * HD)
    result = jnp.clip(jax.random.normal(key, shape, jnp.float32), -6.0, 6.0)
    return result.astype(jnp.bfloat16)


def place_ends(drawn, rng, low, high):
    extent = drawn.shape
    place = [jax.random.randint(jax.random.fold_in(rng, axis), (), 0, extent[axis]) for axis in range(len(extent))]
    drawn = drawn.at[tuple(place)].set(low)
    longest = extent.index(max(extent))
    place[longest] = (place[longest] + 1) % extent[longest]
    return drawn.at[tuple(place)].set(high)


def shard_levels(stream_key, dims, split, smallest, high):
    gain = 1.0
    for dim, shards_of in split:
        heights = jax.random.uniform(jax.random.fold_in(jax.random.fold_in(stream_key, 6), dim), (shards_of,), jnp.float32, smallest / len(split), high / len(split))
        gain = gain * jnp.repeat(jnp.exp(heights), dims[dim] // shards_of).reshape((-1,) + (1,) * (len(dims) - 1 - dim))
    return gain


def bell_draw(rng, extent, scale, most, pieces=(), kind=jnp.bfloat16):
    loudness = shard_levels(rng, extent, pieces, -0.22, 0.18) if pieces else 1.0
    values = jax.random.normal(rng, extent, jnp.float32) * scale * loudness
    return jnp.minimum(jnp.maximum(values, -most), most).astype(kind)


def setup_inputs(seed: int = 0) -> dict:
    seeds = jax.random.split(jax.random.key(seed), 12)
    window = bell_draw(seeds[0], (WINDOW, FT, D), 1.0, 6.0, ((0, 4), (1, 8)))
    levels = place_ends(jax.random.randint(seeds[1], (WINDOW,), 0, LEVELS), jax.random.fold_in(seeds[1], 1), 0, LEVELS - 1).astype(jnp.int32)
    actions = place_ends(jax.random.randint(seeds[2], (WINDOW,), 0, ACTIONS), jax.random.fold_in(seeds[2], 1), 0, ACTIONS - 1).astype(jnp.int32)
    cache_len = jax.random.randint(seeds[3], (1,), FT, CACHE - FT + 1).astype(jnp.int32)
    level_table = bell_draw(seeds[4], (LEVELS, 3, D), 0.7, 4.0, (), jnp.float32)
    action_table = bell_draw(seeds[5], (ACTIONS, 3, D), 0.7, 4.0, (), jnp.float32)
    w_qkv = bell_draw(seeds[6], (3, D, H * HD), D ** -0.5, 0.078125, ((2, 8),))
    w_out = bell_draw(seeds[7], (H * HD, D), (H * HD) ** -0.5, 0.09375, ((0, 8),))
    cache_keys = draw_cache_keys(jax.random.fold_in(seeds[11], 71), 0)
    cache_values = bell_draw(seeds[9], (CACHE, H * HD), 1.0, 6.0, ((0, 4), (1, 8)))
    fresh_frame = bell_draw(seeds[10], (FT, D), 1.0, 6.0, ((0, 8),))
    return {"window": window, "levels": levels, "actions": actions, "cache_len": cache_len, "level_table": level_table, "action_table": action_table, "w_qkv": w_qkv, "w_out": w_out, "cache_keys": cache_keys, "cache_values": cache_values, "fresh_frame": fresh_frame}


EPS = 1e-06
NEG = -1e+30

def reference(window, levels, actions, cache_len, level_table, action_table, w_qkv, w_out, cache_keys, cache_values, fresh_frame):
    condition = level_table[levels] + action_table[actions]
    shift = condition[:, 0][:, None, :]
    scale = condition[:, 1][:, None, :]
    gate = condition[:, 2][:, None, :]
    base_rows = window.astype(jnp.float32)
    center = base_rows - lax.optimization_barrier(jnp.mean(base_rows, axis=-1, keepdims=True))
    spread = lax.optimization_barrier(jnp.mean(center * center, axis=-1, keepdims=True))
    normed = (center * lax.rsqrt(spread + EPS) * (1.0 + scale) + shift).astype(jnp.bfloat16)
    flat = normed.reshape(WINDOW * FT, D)
    projected = [jnp.dot(flat, w_qkv[index], preferred_element_type=jnp.float32).astype(jnp.bfloat16) for index in range(3)]
    query, key, value = [item.reshape(WINDOW, FT, H, HD).transpose(2, 0, 1, 3) for item in projected]
    past_keys = cache_keys.reshape(CACHE, H, HD).transpose(1, 0, 2)
    past_values = cache_values.reshape(CACHE, H, HD).transpose(1, 0, 2)
    length = cache_len[0]
    past_valid = jnp.arange(CACHE, dtype=jnp.int32) < length
    factor = 1.0 / math.sqrt(HD)

    def one_head(inputs):
        queries, keys_now, values_now, keys_past, values_past = inputs
        all_keys = jnp.concatenate([keys_past, keys_now.reshape(WINDOW * FT, HD)], 0)
        all_values = jnp.concatenate([values_past, values_now.reshape(WINDOW * FT, HD)], 0)
        results = []
        for frame in range(WINDOW):
            valid = jnp.concatenate([past_valid, jnp.repeat(jnp.arange(WINDOW) <= frame, FT)])
            scores = jnp.dot(queries[frame], all_keys.T, preferred_element_type=jnp.float32) * factor
            scores = jnp.where(valid[None, :], scores, NEG)
            peak = lax.optimization_barrier(jnp.max(scores, axis=-1, keepdims=True))
            weights = jnp.where(valid[None, :], jnp.exp(scores - peak), 0.0)
            total = lax.optimization_barrier(jnp.sum(weights, axis=-1, keepdims=True))
            mixed = jnp.dot(weights.astype(jnp.bfloat16), all_values, preferred_element_type=jnp.float32) / total
            results.append(mixed.astype(jnp.bfloat16))
        return jnp.stack(results)
    heads = lax.map(one_head, (query, key, value, past_keys, past_values))
    attended = heads.transpose(1, 2, 0, 3).reshape(WINDOW * FT, H * HD)
    projection = jnp.dot(attended, w_out, preferred_element_type=jnp.float32).reshape(WINDOW, FT, D)
    updated = (base_rows + gate * projection).astype(jnp.bfloat16)
    next_window = jnp.concatenate([updated[1:], fresh_frame[None]], 0)
    finished = updated[0]
    first_keys = key[:, 0].transpose(1, 0, 2).reshape(FT, H * HD)
    first_values = value[:, 0].transpose(1, 0, 2).reshape(FT, H * HD)
    start = length.astype(jnp.int32)
    zero = jnp.zeros((), jnp.int32)
    new_cache_keys = lax.dynamic_update_slice(cache_keys, first_keys, (start, zero))
    new_cache_values = lax.dynamic_update_slice(cache_values, first_values, (start, zero))
    return (next_window, finished, new_cache_keys, new_cache_values)
```

```python
import functools
import math

import jax
import jax.numpy as jnp
from jax import lax
from jax.experimental import pallas as pl
from jax.experimental.pallas import tpu as pltpu
from jax.sharding import PartitionSpec as P

HD = 128


EPS = 1e-06
NEG = -1e30


def passed_along(block, axis, distance):
    devices = range(lax.axis_size(axis))
    route = [(i - distance, i) for i in devices if i - distance in devices]
    return lax.ppermute(block, axis, route)


def spread_2(block, axis, source):
    block = jnp.where(lax.axis_index(axis) == source, block, jnp.zeros_like(block))
    return lax.psum(block, axis)


def lookup(table, picks):
    entries = table.shape[0]
    onehot = (picks[:, None] == jnp.arange(entries, dtype=jnp.int32)[None, :]).astype(jnp.float32)
    return jnp.einsum("fl,lcd->fcd", onehot, table, precision=lax.Precision.HIGHEST)


def split_heads(block, groups):
    return block.reshape(block.shape[0], groups, HD).transpose(1, 0, 2)


def attend(state, queries, keys, values, valid):
    peak, total, accum = state
    scores = jnp.einsum("gqd,gkd->gqk", queries, keys, preferred_element_type=jnp.float32) * (
        1.0 / math.sqrt(HD)
    )
    scores = jnp.where(valid[None, None, :], scores, NEG)
    newest = jnp.maximum(peak, jnp.max(scores, axis=-1))
    weights = jnp.where(valid[None, None, :], jnp.exp(scores - newest[..., None]), 0.0)
    carried = jnp.exp(peak - newest)
    total = total * carried + jnp.sum(weights, axis=-1)
    accum = accum * carried[..., None] + jnp.einsum(
        "gqk,gkd->gqd", weights.astype(jnp.bfloat16), values, preferred_element_type=jnp.float32
    )
    return (newest, total, accum)


def insert_rows(shard, fresh_rows, first, length):
    shard_rows, width = shard.shape
    frame_tokens = fresh_rows.shape[0]
    offset = jnp.clip(length - first, -frame_tokens, shard_rows)
    padding = jnp.zeros((shard_rows, width), shard.dtype)
    padded = jnp.concatenate([padding, fresh_rows, padding], 0)
    placed = lax.dynamic_slice_in_dim(padded, shard_rows - offset, shard_rows, 0)
    position = first + jnp.arange(shard_rows, dtype=jnp.int32)
    inside = (position >= length) & (position < length + frame_tokens)
    return jnp.where(inside[:, None], placed, shard)


def on_device(
    window,
    levels,
    actions,
    cache_len,
    level_table,
    action_table,
    w_qkv,
    w_out,
    cache_keys,
    cache_values,
    fresh_frame,
):
    slot = lax.axis_index("frame")
    slot_count = lax.axis_size("frame")
    condition = (lookup(level_table, levels) + lookup(action_table, actions))[0]
    base_rows = window[0].astype(jnp.float32)
    center = base_rows - jnp.mean(base_rows, axis=-1, keepdims=True)
    spread = jnp.mean(center * center, axis=-1, keepdims=True)
    normed = (center * lax.rsqrt(spread + EPS) * (1.0 + condition[1]) + condition[0]).astype(
        jnp.bfloat16
    )
    packed = jnp.einsum(
        "td,cde->tce",
        lax.all_gather(normed, "fsdp", axis=0, tiled=True),
        w_qkv,
        preferred_element_type=jnp.float32,
    ).astype(jnp.bfloat16)
    frame_tokens = packed.shape[0]
    width = packed.shape[2]
    groups = width // HD
    query_rows = packed[:, 0]
    key_own = packed[:, 1]
    value_own = packed[:, 2]
    query = split_heads(query_rows, groups)
    length = cache_len[0]
    shard_rows = cache_keys.shape[0]
    initial = (
        jnp.full((groups, frame_tokens), NEG, jnp.float32),
        jnp.zeros((groups, frame_tokens), jnp.float32),
        jnp.zeros((groups, frame_tokens, HD), jnp.float32),
    )
    everyone = lax.all_gather(query_rows[None], "frame", axis=0, tiled=True)
    local_keys = split_heads(cache_keys, groups)
    local_values = split_heads(cache_values, groups)
    local_valid = slot * shard_rows + jnp.arange(shard_rows, dtype=jnp.int32) < length

    def one_frame(rows_query):
        return attend(
            initial, split_heads(rows_query, groups), local_keys, local_values, local_valid
        )

    local_peak, local_total, local_accum = lax.map(one_frame, everyone)
    peaks = lax.pmax(local_peak, "frame")
    rescale = jnp.exp(local_peak - peaks)
    sums = (
        lax.psum_scatter(
            (local_total * rescale).astype(jnp.bfloat16), "frame", scatter_dimension=0, tiled=True
        ).astype(jnp.float32),
        lax.psum_scatter(
            (local_accum * rescale[..., None]).astype(jnp.bfloat16),
            "frame",
            scatter_dimension=0,
            tiled=True,
        ).astype(jnp.float32),
    )
    own_peak = lax.dynamic_index_in_dim(peaks, slot, 0, keepdims=False)
    state = (own_peak, sums[0][0], sums[1][0])
    pieces = (
        lax.all_gather(key_own[None], "frame", axis=0, tiled=True),
        lax.all_gather(value_own[None], "frame", axis=0, tiled=True),
    )
    count = pieces[0].shape[0]

    def advance(index, inner):
        keys = lax.dynamic_index_in_dim(pieces[0], index, 0, keepdims=False)
        values = lax.dynamic_index_in_dim(pieces[1], index, 0, keepdims=False)
        allowed = jnp.full((frame_tokens,), index <= slot)
        return attend(inner, query, split_heads(keys, groups), split_heads(values, groups), allowed)

    peak, total, accum = lax.fori_loop(0, count, advance, state)
    attended = (
        (accum / total[..., None])
        .astype(jnp.bfloat16)
        .transpose(1, 0, 2)
        .reshape(frame_tokens, width)
    )
    projection = lax.psum_scatter(
        jnp.dot(attended, w_out, preferred_element_type=jnp.float32).astype(jnp.bfloat16),
        "fsdp",
        scatter_dimension=0,
        tiled=True,
    ).astype(jnp.float32)
    updated = (base_rows + condition[2] * projection).astype(jnp.bfloat16)
    moved = passed_along(updated, "frame", -1)
    moved = jnp.where(slot == slot_count - 1, fresh_frame, moved)
    root_keys, root_values, finished = (
        spread_2(key_own, "frame", 0),
        spread_2(value_own, "frame", 0),
        spread_2(updated, "frame", 0),
    )
    first = slot * shard_rows
    new_keys = insert_rows(cache_keys, root_keys, first, length)
    new_values = insert_rows(cache_values, root_values, first, length)
    return (moved[None], finished, new_keys, new_values)


MESH = pl.DeviceIdType.MESH
PAIR = 2
VMEM_BYTES = 60 * 1024 * 1024


def fused(
    F,
    N,
    n,
    window,
    levels,
    actions,
    cache_len,
    level_table,
    action_table,
    w_qkv,
    w_out,
    cache_keys,
    cache_values,
    fresh,
    next_out,
    fin_out,
    nk_out,
    nv_out,
    lt_v,
    at_v,
    wq_v,
    wo_v,
    cache_v,
    kc,
    vc,
    gath,
    base_n,
    gate_s,
    gate_n,
    acc,
    qkv_s,
    qkv_r,
    kv_s,
    k0v0,
    att_s,
    att_r,
    part,
    pair,
    y_s,
    y_r,
    zs_r,
    zs_l,
    zr_r,
    zr_l,
    fin_s,
    fin_r,
    new_v,
    loc,
    wq_sem,
    ag_send,
    ag_recv,
    ca_send,
    ca_recv,
    ba_send,
    ba_recv,
    qk_send,
    qk_recv,
    at_send,
    at_recv,
    k0_send,
    k0_recv,
    ys_sem,
    yr_sem,
    zsr_sem,
    zsl_sem,
    zrr_sem,
    zrl_sem,
    fi_send,
    fi_recv,
):
    f = lax.axis_index("frame")
    i = lax.axis_index("fsdp")
    Y = PAIR
    Z = N // Y
    z = lax.div(i, Y)
    y = lax.rem(i, Y)
    T = window.shape[1]
    D = window.shape[2]
    Dc = D // n
    FT = N * T
    R = cache_keys.shape[0]
    C = cache_keys.shape[1]

    def copy(src, dst, ss, rs, frame, shard):
        return pltpu.make_async_remote_copy(
            src_ref=src,
            dst_ref=dst,
            send_sem=ss,
            recv_sem=rs,
            device_id=(frame, shard),
            device_id_type=MESH,
        )

    right, left, across = i + Y, i - Y, z * Y + (1 - y)

    def head_cols(h):
        return pl.ds(pl.multiple_of(h * HD, HD), HD)

    lt_copy = pltpu.make_async_copy(level_table, lt_v, loc.at[0])
    at_copy = pltpu.make_async_copy(action_table, at_v, loc.at[1])
    lt_copy.start()
    at_copy.start()
    wq_copies = [
        pltpu.make_async_copy(
            w_qkv.at[:, pl.ds(c * Dc, Dc), :], wq_v.at[:, pl.ds(c * Dc, Dc), :], wq_sem.at[c]
        )
        for c in range(n)
    ]
    later = [
        pltpu.make_async_copy(w_out, wo_v, loc.at[2]),
        pltpu.make_async_copy(cache_keys, cache_v.at[0], loc.at[3]),
        pltpu.make_async_copy(cache_values, cache_v.at[1], loc.at[4]),
        pltpu.make_async_copy(cache_keys.at[:, head_cols(f)], kc.at[f], loc.at[5]),
        pltpu.make_async_copy(cache_values.at[:, head_cols(f)], vc.at[f], loc.at[6]),
    ]

    barrier = pltpu.get_barrier_semaphore()
    for d in range(1, F):
        pl.semaphore_signal(
            barrier, inc=1, device_id=(lax.rem(f + d, F), i), device_id_type=MESH
        )
    pl.semaphore_signal(barrier, inc=1, device_id=(f, across), device_id_type=MESH)

    @pl.when(z > 0)
    def _():
        pl.semaphore_signal(barrier, inc=1, device_id=(f, left), device_id_type=MESH)

    @pl.when(z < Z - 1)
    def _():
        pl.semaphore_signal(barrier, inc=1, device_id=(f, right), device_id_type=MESH)

    lt_copy.wait()
    at_copy.wait()
    for item in wq_copies:
        item.start()
    for item in later:
        item.start()
    condition = lt_v[levels[0]] + at_v[actions[0]]
    rows = window[0].astype(jnp.float32)
    center = rows - jnp.mean(rows, axis=-1, keepdims=True)
    spread = jnp.mean(center * center, axis=-1, keepdims=True)
    normed = (
        center * lax.rsqrt(spread + EPS) * (1.0 + condition[1:2]) + condition[0:1]
    ).astype(jnp.bfloat16)
    gate_s[...] = condition[2:3]
    for c in range(n):
        gath[c, i] = normed[:, c * Dc : (c + 1) * Dc]

    pl.semaphore_wait(barrier, F + jnp.minimum(z, 1) + jnp.minimum(Z - 1 - z, 1))

    def ag(c, zs, way, target):
        s = zs * Y + y
        return copy(
            gath.at[c, s], gath.at[c, s], ag_send.at[c, zs, way], ag_recv.at[c, s], f, target
        )

    def ag_wait(c, s):
        copy(gath.at[c, s], gath.at[c, s], ag_send.at[c, 0, 0], ag_recv.at[c, s], f, across).wait_recv()

    for c in range(n):

        @pl.when(z < Z - 1)
        def _():
            ag(c, z, 0, right).start()

        @pl.when(z > 0)
        def _():
            ag(c, z, 1, left).start()

        ag(c, z, 2, across).start()

    def cache_copy(which, d):
        k = lax.rem(f + d, F)
        src, dst = ((cache_keys, kc), (cache_values, vc))[which]
        return copy(
            src.at[:, head_cols(k)], dst.at[f], ca_send.at[which, d], ca_recv.at[which, f], k, i
        )

    def cache_arrival(which, d):
        k = lax.rem(f + d, F)
        dst = (kc, vc)[which]
        copy(dst.at[k], dst.at[k], ca_send.at[which, d], ca_recv.at[which, k], k, i).wait_recv()

    before = lax.rem(f + F - 1, F)
    base_copies = [
        copy(window.at[0], base_n, ba_send.at[0], ba_recv.at[0], before, i),
        copy(gate_s, gate_n, ba_send.at[1], ba_recv.at[1], before, i),
    ]
    for which in range(2):
        for d in range(1, F):
            cache_copy(which, d).start()
    for item in base_copies:
        item.start()

    def forward(c):
        for h in range(1, Z):

            @pl.when(z - h >= 0)
            def _():
                zs = z - h
                ag_wait(c, zs * Y + y)

                @pl.when(z < Z - 1)
                def _():
                    ag(c, zs, 0, right).start()

                ag(c, zs, 2, across).start()

            @pl.when(z + h < Z)
            def _():
                zs = z + h
                ag_wait(c, zs * Y + y)

                @pl.when(z > 0)
                def _():
                    ag(c, zs, 1, left).start()

                ag(c, zs, 2, across).start()

    def project(c):
        for zs in range(Z):
            ag_wait(c, zs * Y + (1 - y))
        wq_copies[c].wait()
        tokens = gath[c].reshape(FT, Dc)
        for k in range(3):
            product = jnp.dot(
                tokens, wq_v[k, c * Dc : (c + 1) * Dc, :], preferred_element_type=jnp.float32
            )
            if c > 0:
                product = product + acc[k]
            if c < n - 1:
                acc[k] = product
            else:
                rounded = product.astype(jnp.bfloat16)
                for h in range(F):
                    qkv_s[h, k] = rounded[:, h * HD : (h + 1) * HD]
                if k > 0:
                    kv_s[k - 1] = rounded

    forward(0)
    for c in range(n):
        if c + 1 < n:
            forward(c + 1)
        project(c)

    def qkv_copy(d):
        k = lax.rem(f + d, F)
        return copy(qkv_s.at[k], qkv_r.at[f], qk_send.at[d], qk_recv.at[f], k, i)

    order = [d for d in range(F // 2, F)] + [d for d in range(1, F // 2)]
    for d in order:
        qkv_copy(d).start()
    qkv_r[f] = qkv_s[f]
    for item in later[3:]:
        item.wait()
    for d in range(1, F):
        for which in range(2):
            cache_arrival(which, d)
    length = cache_len[0]
    for d in order:
        k = lax.rem(f + d, F)
        copy(qkv_r.at[k], qkv_r.at[k], qk_send.at[d], qk_recv.at[k], k, i).wait_recv()

    factor = 1.0 / math.sqrt(HD)
    past_valid = lax.broadcasted_iota(jnp.int32, (1, F * R), 1) < length
    dims = (((1,), (1,)), ((), ()))

    def att_copy(d):
        target = lax.rem(f + d, F)
        a = lax.rem(target + 1, F)
        return copy(
            att_s.at[a], att_r.at[:, head_cols(f)], at_send.at[d], at_recv.at[f], target, i
        )

    for d in order + [0]:
        a = lax.rem(f + d + 1, F)
        queries = qkv_r[a, 0]
        past = lax.dot_general(
            queries, kc[...].reshape(F * R, HD), dims, preferred_element_type=jnp.float32
        )
        now = lax.dot_general(
            queries, qkv_r[:, 1].reshape(F * FT, HD), dims, preferred_element_type=jnp.float32
        )
        past = jnp.where(past_valid, past * factor, NEG)
        now_valid = lax.broadcasted_iota(jnp.int32, (1, F * FT), 1) < (a + 1) * FT
        now = jnp.where(now_valid, now * factor, NEG)
        peak = jnp.maximum(
            jnp.max(past, axis=-1, keepdims=True), jnp.max(now, axis=-1, keepdims=True)
        )
        past = jnp.exp(past - peak)
        now = jnp.exp(now - peak)
        total = jnp.sum(past, axis=-1, keepdims=True) + jnp.sum(now, axis=-1, keepdims=True)
        mixed = jnp.dot(
            past.astype(jnp.bfloat16),
            vc[...].reshape(F * R, HD),
            preferred_element_type=jnp.float32,
        ) + jnp.dot(
            now.astype(jnp.bfloat16),
            qkv_r[:, 2].reshape(F * FT, HD),
            preferred_element_type=jnp.float32,
        )
        result = (mixed / total).astype(jnp.bfloat16)
        if d == 0:
            att_r[:, head_cols(f)] = result
        else:
            att_s[a] = result
            att_copy(d).start()

    def k0_copy(d):
        return copy(kv_s, k0v0, k0_send.at[d], k0_recv.at[0], lax.rem(f + d, F), i)

    @pl.when(f == 0)
    def _():
        for d in range(1, F):
            k0_copy(d).start()
        k0v0[...] = kv_s[...]

    later[0].wait()
    for d in order:
        k = lax.rem(f + d, F)
        cols = att_r.at[:, head_cols(k)]
        copy(cols, cols, at_send.at[d], at_recv.at[k], k, i).wait_recv()

    def y_copy(c):
        return copy(y_s.at[c], y_r.at[c], ys_sem.at[c], yr_sem.at[c], f, across)

    def right_copy(c, zd):
        return copy(zs_r.at[c, zd], zr_r.at[c, zd], zsr_sem.at[c, zd], zrr_sem.at[c, zd], f, right)

    def left_copy(c, zd):
        return copy(zs_l.at[c, zd], zr_l.at[c, zd], zsl_sem.at[c, zd], zrl_sem.at[c, zd], f, left)

    def fin_copy(c, d):
        return copy(
            fin_s.at[c], fin_r.at[c], fi_send.at[c, d], fi_recv.at[c], lax.rem(f + d, F), i
        )

    def multiply(c):
        part[...] = jnp.dot(
            att_r[...], wo_v[:, c * Dc : (c + 1) * Dc], preferred_element_type=jnp.float32
        ).reshape(N, T, Dc)
        for zd in range(Z):
            y_s[c, zd] = part[zd * Y + (1 - y)].astype(jnp.bfloat16)
        y_copy(c).start()
        for zd in range(Z):
            pair[c, zd] = part[zd * Y + y]

    def add_pair(c):
        y_copy(c).wait_recv()
        pair[c] = pair[c] + y_r[c].astype(jnp.float32)

    def line(c, k):
        @pl.when(z == k)
        def _():
            for zd in range(Z - 1, k, -1):
                value = pair[c, zd]
                if k > 0:
                    right_copy(c, zd).wait_recv()
                    value = value + zr_r[c, zd].astype(jnp.float32)
                zs_r[c, zd] = value.astype(jnp.bfloat16)
                right_copy(c, zd).start()

        @pl.when(z == Z - 1 - k)
        def _():
            for zd in range(Z - 1 - k):
                value = pair[c, zd]
                if k > 0:
                    left_copy(c, zd).wait_recv()
                    value = value + zr_l[c, zd].astype(jnp.float32)
                zs_l[c, zd] = value.astype(jnp.bfloat16)
                left_copy(c, zd).start()

    def finish(c):
        @pl.when(z > 0)
        def _():
            right_copy(c, z).wait_recv()
            pair[c, z] = pair[c, z] + zr_r[c, z].astype(jnp.float32)

        @pl.when(z < Z - 1)
        def _():
            left_copy(c, z).wait_recv()
            pair[c, z] = pair[c, z] + zr_l[c, z].astype(jnp.float32)

        cols = slice(c * Dc, (c + 1) * Dc)
        updated = (base_n[:, cols].astype(jnp.float32) + gate_n[:, cols] * pair[c, z]).astype(
            jnp.bfloat16
        )

        @pl.when(f < F - 1)
        def _():
            next_out[0, :, cols] = updated

        @pl.when(f == F - 1)
        def _():
            fin_s[c] = updated
            for d in range(1, F):
                fin_copy(c, d).start()
            fin_out[:, cols] = updated

    new_copies = [
        pltpu.make_async_copy(new_v.at[0], nk_out, loc.at[7]),
        pltpu.make_async_copy(new_v.at[1], nv_out, loc.at[8]),
    ]

    def insert():
        @pl.when(f != 0)
        def _():
            k0_copy(1).wait_recv()

        row = lax.broadcasted_iota(jnp.int32, (R, FT), 0) + (f * R - length)
        pick = jnp.where(row == lax.broadcasted_iota(jnp.int32, (R, FT), 1), 1.0, 0.0).astype(
            jnp.bfloat16
        )
        position = lax.broadcasted_iota(jnp.int32, (R, C), 0) + (f * R - length)
        inside = (position >= 0) & (position < FT)
        for k in range(2):
            later[1 + k].wait()
            placed = jnp.dot(pick, k0v0[k], preferred_element_type=jnp.float32)
            new_v[k] = jnp.where(inside, placed, cache_v[k].astype(jnp.float32)).astype(
                jnp.bfloat16
            )
            new_copies[k].start()

    @pl.when(f == F - 1)
    def _():
        next_out[0] = fresh[...]

    for step in range(n + Z):
        if step < n:
            multiply(step)
        if step == 0:
            for item in base_copies:
                item.wait_recv()
        if 0 <= step - 1 < n:
            add_pair(step - 1)
        for k in range(Z - 1):
            if 0 <= step - 1 - k < n:
                line(step - 1 - k, k)
        if step == n:
            insert()
        if 0 <= step - Z < n:
            finish(step - Z)

    @pl.when(f < F - 1)
    def _():
        for c in range(n):
            fin_copy(c, 1).wait_recv()
            fin_out[:, c * Dc : (c + 1) * Dc] = fin_r[c]

    for c in range(n):
        for zs in range(Z):

            @pl.when((zs <= z) & (z < Z - 1))
            def _():
                ag(c, zs, 0, right).wait_send()

            @pl.when((zs >= z) & (z > 0))
            def _():
                ag(c, zs, 1, left).wait_send()

            ag(c, zs, 2, across).wait_send()

            @pl.when(z < zs)
            def _():
                right_copy(c, zs).wait_send()

            @pl.when(z > zs)
            def _():
                left_copy(c, zs).wait_send()

        y_copy(c).wait_send()
    for d in range(1, F):
        for which in range(2):
            cache_copy(which, d).wait_send()
        qkv_copy(d).wait_send()
        att_copy(d).wait_send()
    for item in base_copies:
        item.wait_send()

    @pl.when(f == 0)
    def _():
        for d in range(1, F):
            k0_copy(d).wait_send()

    @pl.when(f == F - 1)
    def _():
        for c in range(n):
            for d in range(1, F):
                fin_copy(c, d).wait_send()

    for item in new_copies:
        item.wait()


def pieces_of(width):
    return next(k for k in (4, 5, 2, 1) if width % (k * HD) == 0)


def fused_call(mesh, *args):
    window, _, _, _, level_table, action_table, w_qkv, w_out, cache_keys, cache_values, _ = args
    F, N = mesh.shape["frame"], mesh.shape["fsdp"]
    T, D = window.shape[1:]
    R, C = cache_keys.shape
    FT = N * T
    Z = N // PAIR
    n = pieces_of(D)
    Dc = D // n
    bf, f32 = jnp.bfloat16, jnp.float32
    vmem = pl.BlockSpec(memory_space=pltpu.VMEM)
    smem = pl.BlockSpec(memory_space=pltpu.SMEM)
    anys = pl.BlockSpec(memory_space=pl.ANY)
    dma = pltpu.SemaphoreType.DMA
    scratch = [
        pltpu.VMEM(level_table.shape, f32),
        pltpu.VMEM(action_table.shape, f32),
        pltpu.VMEM(w_qkv.shape, bf),
        pltpu.VMEM(w_out.shape, bf),
        pltpu.VMEM((2, R, C), bf),
        pltpu.VMEM((F, R, HD), bf),
        pltpu.VMEM((F, R, HD), bf),
        pltpu.VMEM((n, N, T, Dc), bf),
        pltpu.VMEM((T, D), bf),
        pltpu.VMEM((1, D), f32),
        pltpu.VMEM((1, D), f32),
        pltpu.VMEM((3, FT, C), f32),
        pltpu.VMEM((F, 3, FT, HD), bf),
        pltpu.VMEM((F, 3, FT, HD), bf),
        pltpu.VMEM((2, FT, C), bf),
        pltpu.VMEM((2, FT, C), bf),
        pltpu.VMEM((F, FT, HD), bf),
        pltpu.VMEM((FT, C), bf),
        pltpu.VMEM((N, T, Dc), f32),
        pltpu.VMEM((n, Z, T, Dc), f32),
        pltpu.VMEM((n, Z, T, Dc), bf),
        pltpu.VMEM((n, Z, T, Dc), bf),
        pltpu.VMEM((n, Z, T, Dc), bf),
        pltpu.VMEM((n, Z, T, Dc), bf),
        pltpu.VMEM((n, Z, T, Dc), bf),
        pltpu.VMEM((n, Z, T, Dc), bf),
        pltpu.VMEM((n, T, Dc), bf),
        pltpu.VMEM((n, T, Dc), bf),
        pltpu.VMEM((2, R, C), bf),
        dma((9,)),
        dma((n,)),
        dma((n, Z, 3)),
        dma((n, N)),
        dma((2, F)),
        dma((2, F)),
        dma((2,)),
        dma((2,)),
        dma((F,)),
        dma((F,)),
        dma((F,)),
        dma((F,)),
        dma((F,)),
        dma((1,)),
        dma((n,)),
        dma((n,)),
        dma((n, Z)),
        dma((n, Z)),
        dma((n, Z)),
        dma((n, Z)),
        dma((n, F)),
        dma((n,)),
    ]
    return pl.pallas_call(
        functools.partial(fused, F, N, n),
        out_shape=(
            jax.ShapeDtypeStruct(window.shape, bf),
            jax.ShapeDtypeStruct(window.shape[1:], bf),
            jax.ShapeDtypeStruct(cache_keys.shape, bf),
            jax.ShapeDtypeStruct(cache_values.shape, bf),
        ),
        in_specs=[vmem, smem, smem, smem, anys, anys, anys, anys, anys, anys, vmem],
        out_specs=(vmem, vmem, anys, anys),
        scratch_shapes=scratch,
        compiler_params=pltpu.CompilerParams(
            collective_id=0, has_side_effects=True, vmem_limit_bytes=VMEM_BYTES
        ),
    )(*args)


def dispatch(mesh, *args):
    window, w_qkv, cache_keys = args[0], args[6], args[8]
    F, N = mesh.shape["frame"], mesh.shape["fsdp"]
    heads = w_qkv.shape[2] // HD
    suits = (
        tuple(mesh.axis_names) == ("frame", "fsdp")
        and F > 1
        and heads == F
        and window.shape[0] == 1
        and N % PAIR == 0
        and window.shape[1] % 16 == 0
        and cache_keys.shape[0] % 16 == 0
    )
    if suits:
        return fused_call(mesh, *args)
    return on_device(*args)


def solution(mesh):
    in_specs = (
        P("frame", "fsdp", None),
        P("frame"),
        P("frame"),
        P(),
        P(),
        P(),
        P(None, None, "fsdp"),
        P("fsdp", None),
        P("frame", "fsdp"),
        P("frame", "fsdp"),
        P("fsdp", None),
    )
    out_specs = (P("frame", "fsdp", None), P("fsdp", None), P("frame", "fsdp"), P("frame", "fsdp"))
    return jax.shard_map(
        functools.partial(dispatch, mesh), mesh=mesh, in_specs=in_specs, out_specs=out_specs, check_vma=False
    )
```

```python
import functools
import math

import jax
import jax.numpy as jnp
from jax import lax
from jax.experimental import pallas as pl
from jax.experimental.pallas import tpu as pltpu
from jax.sharding import PartitionSpec as P

HD = 128


EPS = 1e-06
NEG = -1e30


def passed_along(block, axis, distance):
    devices = range(lax.axis_size(axis))
    route = [(i - distance, i) for i in devices if i - distance in devices]
    return lax.ppermute(block, axis, route)


def spread_2(block, axis, source):
    block = jnp.where(lax.axis_index(axis) == source, block, jnp.zeros_like(block))
    return lax.psum(block, axis)


def lookup(table, picks):
    entries = table.shape[0]
    onehot = (picks[:, None] == jnp.arange(entries, dtype=jnp.int32)[None, :]).astype(jnp.float32)
    return jnp.einsum("fl,lcd->fcd", onehot, table, precision=lax.Precision.HIGHEST)


def split_heads(block, groups):
    return block.reshape(block.shape[0], groups, HD).transpose(1, 0, 2)


def attend(state, queries, keys, values, valid):
    peak, total, accum = state
    scores = jnp.einsum("gqd,gkd->gqk", queries, keys, preferred_element_type=jnp.float32) * (
        1.0 / math.sqrt(HD)
    )
    scores = jnp.where(valid[None, None, :], scores, NEG)
    newest = jnp.maximum(peak, jnp.max(scores, axis=-1))
    weights = jnp.where(valid[None, None, :], jnp.exp(scores - newest[..., None]), 0.0)
    carried = jnp.exp(peak - newest)
    total = total * carried + jnp.sum(weights, axis=-1)
    accum = accum * carried[..., None] + jnp.einsum(
        "gqk,gkd->gqd", weights.astype(jnp.bfloat16), values, preferred_element_type=jnp.float32
    )
    return (newest, total, accum)


def insert_rows(shard, fresh_rows, first, length):
    shard_rows, width = shard.shape
    frame_tokens = fresh_rows.shape[0]
    offset = jnp.clip(length - first, -frame_tokens, shard_rows)
    padding = jnp.zeros((shard_rows, width), shard.dtype)
    padded = jnp.concatenate([padding, fresh_rows, padding], 0)
    placed = lax.dynamic_slice_in_dim(padded, shard_rows - offset, shard_rows, 0)
    position = first + jnp.arange(shard_rows, dtype=jnp.int32)
    inside = (position >= length) & (position < length + frame_tokens)
    return jnp.where(inside[:, None], placed, shard)


def on_device(
    window,
    levels,
    actions,
    cache_len,
    level_table,
    action_table,
    w_qkv,
    w_out,
    cache_keys,
    cache_values,
    fresh_frame,
):
    slot = lax.axis_index("frame")
    slot_count = lax.axis_size("frame")
    condition = (lookup(level_table, levels) + lookup(action_table, actions))[0]
    base_rows = window[0].astype(jnp.float32)
    center = base_rows - jnp.mean(base_rows, axis=-1, keepdims=True)
    spread = jnp.mean(center * center, axis=-1, keepdims=True)
    normed = (center * lax.rsqrt(spread + EPS) * (1.0 + condition[1]) + condition[0]).astype(
        jnp.bfloat16
    )
    packed = jnp.einsum(
        "td,cde->tce",
        lax.all_gather(normed, "fsdp", axis=0, tiled=True),
        w_qkv,
        preferred_element_type=jnp.float32,
    ).astype(jnp.bfloat16)
    frame_tokens = packed.shape[0]
    width = packed.shape[2]
    groups = width // HD
    query_rows = packed[:, 0]
    key_own = packed[:, 1]
    value_own = packed[:, 2]
    query = split_heads(query_rows, groups)
    length = cache_len[0]
    shard_rows = cache_keys.shape[0]
    initial = (
        jnp.full((groups, frame_tokens), NEG, jnp.float32),
        jnp.zeros((groups, frame_tokens), jnp.float32),
        jnp.zeros((groups, frame_tokens, HD), jnp.float32),
    )
    everyone = lax.all_gather(query_rows[None], "frame", axis=0, tiled=True)
    local_keys = split_heads(cache_keys, groups)
    local_values = split_heads(cache_values, groups)
    local_valid = slot * shard_rows + jnp.arange(shard_rows, dtype=jnp.int32) < length

    def one_frame(rows_query):
        return attend(
            initial, split_heads(rows_query, groups), local_keys, local_values, local_valid
        )

    local_peak, local_total, local_accum = lax.map(one_frame, everyone)
    peaks = lax.pmax(local_peak, "frame")
    rescale = jnp.exp(local_peak - peaks)
    sums = (
        lax.psum_scatter(
            (local_total * rescale).astype(jnp.bfloat16), "frame", scatter_dimension=0, tiled=True
        ).astype(jnp.float32),
        lax.psum_scatter(
            (local_accum * rescale[..., None]).astype(jnp.bfloat16),
            "frame",
            scatter_dimension=0,
            tiled=True,
        ).astype(jnp.float32),
    )
    own_peak = lax.dynamic_index_in_dim(peaks, slot, 0, keepdims=False)
    state = (own_peak, sums[0][0], sums[1][0])
    pieces = (
        lax.all_gather(key_own[None], "frame", axis=0, tiled=True),
        lax.all_gather(value_own[None], "frame", axis=0, tiled=True),
    )
    count = pieces[0].shape[0]

    def advance(index, inner):
        keys = lax.dynamic_index_in_dim(pieces[0], index, 0, keepdims=False)
        values = lax.dynamic_index_in_dim(pieces[1], index, 0, keepdims=False)
        allowed = jnp.full((frame_tokens,), index <= slot)
        return attend(inner, query, split_heads(keys, groups), split_heads(values, groups), allowed)

    peak, total, accum = lax.fori_loop(0, count, advance, state)
    attended = (
        (accum / total[..., None])
        .astype(jnp.bfloat16)
        .transpose(1, 0, 2)
        .reshape(frame_tokens, width)
    )
    projection = lax.psum_scatter(
        jnp.dot(attended, w_out, preferred_element_type=jnp.float32).astype(jnp.bfloat16),
        "fsdp",
        scatter_dimension=0,
        tiled=True,
    ).astype(jnp.float32)
    updated = (base_rows + condition[2] * projection).astype(jnp.bfloat16)
    moved = passed_along(updated, "frame", -1)
    moved = jnp.where(slot == slot_count - 1, fresh_frame, moved)
    root_keys, root_values, finished = (
        spread_2(key_own, "frame", 0),
        spread_2(value_own, "frame", 0),
        spread_2(updated, "frame", 0),
    )
    first = slot * shard_rows
    new_keys = insert_rows(cache_keys, root_keys, first, length)
    new_values = insert_rows(cache_values, root_values, first, length)
    return (moved[None], finished, new_keys, new_values)


MESH = pl.DeviceIdType.MESH
PAIR = 2
VMEM_BYTES = 60 * 1024 * 1024


def fused(
    F,
    N,
    n,
    window,
    levels,
    actions,
    cache_len,
    level_table,
    action_table,
    w_qkv,
    w_out,
    cache_keys,
    cache_values,
    fresh,
    next_out,
    fin_out,
    nk_out,
    nv_out,
    lt_v,
    at_v,
    wq_v,
    wo_v,
    cache_v,
    kc,
    vc,
    gath,
    base_n,
    gate_s,
    gate_n,
    acc,
    qkv_s,
    qkv_r,
    kv_s,
    k0v0,
    att_s,
    att_r,
    part,
    pair,
    y_s,
    y_r,
    zs_r,
    zs_l,
    zr_r,
    zr_l,
    fin_s,
    fin_r,
    new_v,
    loc,
    wq_sem,
    ag_send,
    ag_recv,
    ca_send,
    ca_recv,
    ba_send,
    ba_recv,
    qk_send,
    qk_recv,
    at_send,
    at_recv,
    k0_send,
    k0_recv,
    ys_sem,
    yr_sem,
    zsr_sem,
    zsl_sem,
    zrr_sem,
    zrl_sem,
    fi_send,
    fi_recv,
):
    f = lax.axis_index("frame")
    i = lax.axis_index("fsdp")
    Y = PAIR
    Z = N // Y
    z = lax.div(i, Y)
    y = lax.rem(i, Y)
    T = window.shape[1]
    D = window.shape[2]
    Dc = D // n
    FT = N * T
    R = cache_keys.shape[0]
    C = cache_keys.shape[1]

    def copy(src, dst, ss, rs, frame, shard):
        return pltpu.make_async_remote_copy(
            src_ref=src,
            dst_ref=dst,
            send_sem=ss,
            recv_sem=rs,
            device_id=(frame, shard),
            device_id_type=MESH,
        )

    right, left, across = i + Y, i - Y, z * Y + (1 - y)

    def head_cols(h):
        return pl.ds(pl.multiple_of(h * HD, HD), HD)

    lt_copy = pltpu.make_async_copy(level_table, lt_v, loc.at[0])
    at_copy = pltpu.make_async_copy(action_table, at_v, loc.at[1])
    lt_copy.start()
    at_copy.start()
    wq_copies = [
        pltpu.make_async_copy(
            w_qkv.at[:, pl.ds(c * Dc, Dc), :], wq_v.at[:, pl.ds(c * Dc, Dc), :], wq_sem.at[c]
        )
        for c in range(n)
    ]
    later = [
        pltpu.make_async_copy(w_out, wo_v, loc.at[2]),
        pltpu.make_async_copy(cache_keys, cache_v.at[0], loc.at[3]),
        pltpu.make_async_copy(cache_values, cache_v.at[1], loc.at[4]),
        pltpu.make_async_copy(cache_keys.at[:, head_cols(f)], kc.at[f], loc.at[5]),
        pltpu.make_async_copy(cache_values.at[:, head_cols(f)], vc.at[f], loc.at[6]),
    ]

    barrier = pltpu.get_barrier_semaphore()
    for d in range(1, F):
        pl.semaphore_signal(
            barrier, inc=1, device_id=(lax.rem(f + d, F), i), device_id_type=MESH
        )
    pl.semaphore_signal(barrier, inc=1, device_id=(f, across), device_id_type=MESH)

    @pl.when(z > 0)
    def _():
        pl.semaphore_signal(barrier, inc=1, device_id=(f, left), device_id_type=MESH)

    @pl.when(z < Z - 1)
    def _():
        pl.semaphore_signal(barrier, inc=1, device_id=(f, right), device_id_type=MESH)

    lt_copy.wait()
    at_copy.wait()
    for item in wq_copies:
        item.start()
    for item in later:
        item.start()
    level, action = levels[0], actions[0]
    condition = [lt_v[k, pl.ds(level, 1), :] + at_v[k, pl.ds(action, 1), :] for k in range(3)]
    rows = window[0].astype(jnp.float32)
    center = rows - jnp.mean(rows, axis=-1, keepdims=True)
    spread = jnp.mean(center * center, axis=-1, keepdims=True)
    normed = (
        center * lax.rsqrt(spread + EPS) * (1.0 + condition[1]) + condition[0]
    ).astype(jnp.bfloat16)
    gate_s[...] = condition[2]
    for c in range(n):
        gath[c, i] = normed[:, c * Dc : (c + 1) * Dc]

    pl.semaphore_wait(barrier, F + jnp.minimum(z, 1) + jnp.minimum(Z - 1 - z, 1))

    def ag(c, zs, way, target):
        s = zs * Y + y
        return copy(
            gath.at[c, s], gath.at[c, s], ag_send.at[c, zs, way], ag_recv.at[c, s], f, target
        )

    def ag_wait(c, s):
        copy(gath.at[c, s], gath.at[c, s], ag_send.at[c, 0, 0], ag_recv.at[c, s], f, across).wait_recv()

    for c in range(n):

        @pl.when(z < Z - 1)
        def _():
            ag(c, z, 0, right).start()

        @pl.when(z > 0)
        def _():
            ag(c, z, 1, left).start()

        ag(c, z, 2, across).start()

    def cache_copy(which, d):
        k = lax.rem(f + d, F)
        src, dst = ((cache_keys, kc), (cache_values, vc))[which]
        return copy(
            src.at[:, head_cols(k)], dst.at[f], ca_send.at[which, d], ca_recv.at[which, f], k, i
        )

    def cache_arrival(which, d):
        k = lax.rem(f + d, F)
        dst = (kc, vc)[which]
        copy(dst.at[k], dst.at[k], ca_send.at[which, d], ca_recv.at[which, k], k, i).wait_recv()

    before = lax.rem(f + F - 1, F)
    base_copies = [
        copy(window.at[0], base_n, ba_send.at[0], ba_recv.at[0], before, i),
        copy(gate_s, gate_n, ba_send.at[1], ba_recv.at[1], before, i),
    ]
    for which in range(2):
        for d in range(1, F):
            cache_copy(which, d).start()
    for item in base_copies:
        item.start()

    def forward(c):
        for h in range(1, Z):

            @pl.when(z - h >= 0)
            def _():
                zs = z - h
                ag_wait(c, zs * Y + y)

                @pl.when(z < Z - 1)
                def _():
                    ag(c, zs, 0, right).start()

                ag(c, zs, 2, across).start()

            @pl.when(z + h < Z)
            def _():
                zs = z + h
                ag_wait(c, zs * Y + y)

                @pl.when(z > 0)
                def _():
                    ag(c, zs, 1, left).start()

                ag(c, zs, 2, across).start()

    def project(c):
        for zs in range(Z):
            ag_wait(c, zs * Y + (1 - y))
        wq_copies[c].wait()
        tokens = gath[c].reshape(FT, Dc)
        for k in range(3):
            product = jnp.dot(
                tokens, wq_v[k, c * Dc : (c + 1) * Dc, :], preferred_element_type=jnp.float32
            )
            if c > 0:
                product = product + acc[k]
            if c < n - 1:
                acc[k] = product
            else:
                rounded = product.astype(jnp.bfloat16)
                for h in range(F):
                    qkv_s[h, k] = rounded[:, h * HD : (h + 1) * HD]
                if k > 0:
                    kv_s[k - 1] = rounded

    forward(0)
    for c in range(n):
        if c + 1 < n:
            forward(c + 1)
        project(c)

    def qkv_copy(d):
        k = lax.rem(f + d, F)
        return copy(qkv_s.at[k], qkv_r.at[f], qk_send.at[d], qk_recv.at[f], k, i)

    order = [d for d in range(F // 2, F)] + [d for d in range(1, F // 2)]
    for d in order:
        qkv_copy(d).start()
    qkv_r[f] = qkv_s[f]
    for item in later[3:]:
        item.wait()
    for d in range(1, F):
        for which in range(2):
            cache_arrival(which, d)
    length = cache_len[0]
    for d in order:
        k = lax.rem(f + d, F)
        copy(qkv_r.at[k], qkv_r.at[k], qk_send.at[d], qk_recv.at[k], k, i).wait_recv()

    def k0_copy(d):
        return copy(kv_s, k0v0, k0_send.at[d], k0_recv.at[0], lax.rem(f + d, F), i)

    @pl.when(f == 0)
    def _():
        for d in range(1, F):
            k0_copy(d).start()
        k0v0[...] = kv_s[...]

    factor = math.log2(math.e) / math.sqrt(HD)
    past_valid = lax.broadcasted_iota(jnp.int32, (1, F * R), 1) < length
    dims = (((1,), (1,)), ((), ()))

    def att_copy(d):
        target = lax.rem(f + d, F)
        a = lax.rem(target + 1, F)
        return copy(
            att_s.at[a], att_r.at[:, head_cols(f)], at_send.at[d], at_recv.at[f], target, i
        )

    everything = order + [0]
    half = max(1, F // 2)
    for group in [everything[at : at + half] for at in range(0, F, half)]:
        frames = [lax.rem(f + d + 1, F) for d in group]
        queries = jnp.concatenate([qkv_r[a, 0] for a in frames], 0)
        past = lax.dot_general(
            queries, kc[...].reshape(F * R, HD), dims, preferred_element_type=jnp.float32
        )
        now = lax.dot_general(
            queries, qkv_r[:, 1].reshape(F * FT, HD), dims, preferred_element_type=jnp.float32
        )
        past = jnp.where(past_valid, past, NEG)
        token = lax.broadcasted_iota(jnp.int32, (FT, F * FT), 1)
        now = jnp.concatenate(
            [
                jnp.where(token < (a + 1) * FT, now[at * FT : (at + 1) * FT], NEG)
                for at, a in enumerate(frames)
            ],
            0,
        )
        peak = jnp.maximum(
            jnp.max(past, axis=-1, keepdims=True), jnp.max(now, axis=-1, keepdims=True)
        )
        past = jnp.exp2((past - peak) * factor)
        now = jnp.exp2((now - peak) * factor)
        total = jnp.sum(past, axis=-1, keepdims=True) + jnp.sum(now, axis=-1, keepdims=True)
        mixed = jnp.dot(
            past.astype(jnp.bfloat16),
            vc[...].reshape(F * R, HD),
            preferred_element_type=jnp.float32,
        ) + jnp.dot(
            now.astype(jnp.bfloat16),
            qkv_r[:, 2].reshape(F * FT, HD),
            preferred_element_type=jnp.float32,
        )
        result = (mixed / total).astype(jnp.bfloat16)
        for at, d in enumerate(group):
            own = result[at * FT : (at + 1) * FT]
            if d == 0:
                att_r[:, head_cols(f)] = own
            else:
                att_s[frames[at]] = own
                att_copy(d).start()

    new_copies = [
        pltpu.make_async_copy(new_v.at[0], nk_out, loc.at[7]),
        pltpu.make_async_copy(new_v.at[1], nv_out, loc.at[8]),
    ]

    def insert():
        @pl.when(f != 0)
        def _():
            k0_copy(1).wait_recv()

        row = lax.broadcasted_iota(jnp.int32, (R, FT), 0) + (f * R - length)
        pick = jnp.where(row == lax.broadcasted_iota(jnp.int32, (R, FT), 1), 1.0, 0.0).astype(
            jnp.bfloat16
        )
        position = lax.broadcasted_iota(jnp.int32, (R, C), 0) + (f * R - length)
        inside = (position >= 0) & (position < FT)
        for k in range(2):
            later[1 + k].wait()
            placed = jnp.dot(pick, k0v0[k], preferred_element_type=jnp.float32)
            new_v[k] = jnp.where(inside, placed, cache_v[k].astype(jnp.float32)).astype(
                jnp.bfloat16
            )
            new_copies[k].start()

    insert()
    later[0].wait()
    for d in order:
        k = lax.rem(f + d, F)
        cols = att_r.at[:, head_cols(k)]
        copy(cols, cols, at_send.at[d], at_recv.at[k], k, i).wait_recv()

    def y_copy(c):
        return copy(y_s.at[c], y_r.at[c], ys_sem.at[c], yr_sem.at[c], f, across)

    def right_copy(c, zd):
        return copy(zs_r.at[c, zd], zr_r.at[c, zd], zsr_sem.at[c, zd], zrr_sem.at[c, zd], f, right)

    def left_copy(c, zd):
        return copy(zs_l.at[c, zd], zr_l.at[c, zd], zsl_sem.at[c, zd], zrl_sem.at[c, zd], f, left)

    def fin_copy(c, d):
        return copy(
            fin_s.at[c], fin_r.at[c], fi_send.at[c, d], fi_recv.at[c], lax.rem(f + d, F), i
        )

    def multiply(c):
        part[...] = jnp.dot(
            att_r[...], wo_v[:, c * Dc : (c + 1) * Dc], preferred_element_type=jnp.float32
        ).reshape(N, T, Dc)
        for zd in range(Z):
            y_s[c, zd] = part[zd * Y + (1 - y)].astype(jnp.bfloat16)
        y_copy(c).start()
        for zd in range(Z):
            pair[c, zd] = part[zd * Y + y]

    def add_pair(c):
        y_copy(c).wait_recv()
        pair[c] = pair[c] + y_r[c].astype(jnp.float32)

    def line(c, k):
        @pl.when(z == k)
        def _():
            for zd in range(Z - 1, k, -1):
                value = pair[c, zd]
                if k > 0:
                    right_copy(c, zd).wait_recv()
                    value = value + zr_r[c, zd].astype(jnp.float32)
                zs_r[c, zd] = value.astype(jnp.bfloat16)
                right_copy(c, zd).start()

        @pl.when(z == Z - 1 - k)
        def _():
            for zd in range(Z - 1 - k):
                value = pair[c, zd]
                if k > 0:
                    left_copy(c, zd).wait_recv()
                    value = value + zr_l[c, zd].astype(jnp.float32)
                zs_l[c, zd] = value.astype(jnp.bfloat16)
                left_copy(c, zd).start()

    def finish(c):
        @pl.when(z > 0)
        def _():
            right_copy(c, z).wait_recv()
            pair[c, z] = pair[c, z] + zr_r[c, z].astype(jnp.float32)

        @pl.when(z < Z - 1)
        def _():
            left_copy(c, z).wait_recv()
            pair[c, z] = pair[c, z] + zr_l[c, z].astype(jnp.float32)

        cols = slice(c * Dc, (c + 1) * Dc)
        updated = (base_n[:, cols].astype(jnp.float32) + gate_n[:, cols] * pair[c, z]).astype(
            jnp.bfloat16
        )

        @pl.when(f < F - 1)
        def _():
            next_out[0, :, cols] = updated

        @pl.when(f == F - 1)
        def _():
            fin_s[c] = updated
            for d in range(1, F):
                fin_copy(c, d).start()
            fin_out[:, cols] = updated

    @pl.when(f == F - 1)
    def _():
        next_out[0] = fresh[...]

    for step in range(n + Z):
        if step < n:
            multiply(step)
        if step == 0:
            for item in base_copies:
                item.wait_recv()
        if 0 <= step - 1 < n:
            add_pair(step - 1)
        for k in range(Z - 1):
            if 0 <= step - 1 - k < n:
                line(step - 1 - k, k)
        if 0 <= step - Z < n:
            finish(step - Z)

    @pl.when(f < F - 1)
    def _():
        for c in range(n):
            fin_copy(c, 1).wait_recv()
            fin_out[:, c * Dc : (c + 1) * Dc] = fin_r[c]

    for c in range(n):
        for zs in range(Z):

            @pl.when((zs <= z) & (z < Z - 1))
            def _():
                ag(c, zs, 0, right).wait_send()

            @pl.when((zs >= z) & (z > 0))
            def _():
                ag(c, zs, 1, left).wait_send()

            ag(c, zs, 2, across).wait_send()

            @pl.when(z < zs)
            def _():
                right_copy(c, zs).wait_send()

            @pl.when(z > zs)
            def _():
                left_copy(c, zs).wait_send()

        y_copy(c).wait_send()
    for d in range(1, F):
        for which in range(2):
            cache_copy(which, d).wait_send()
        qkv_copy(d).wait_send()
        att_copy(d).wait_send()
    for item in base_copies:
        item.wait_send()

    @pl.when(f == 0)
    def _():
        for d in range(1, F):
            k0_copy(d).wait_send()

    @pl.when(f == F - 1)
    def _():
        for c in range(n):
            for d in range(1, F):
                fin_copy(c, d).wait_send()

    for item in new_copies:
        item.wait()


def hand_out(*refs):
    sources, targets, sems = refs[:4], refs[4:8], refs[8]
    copies = [
        pltpu.make_async_copy(source, target, sems.at[k])
        for k, (source, target) in enumerate(zip(sources, targets))
    ]
    for item in copies:
        item.start()
    for item in copies:
        item.wait()


def pieces_of(width):
    return next(k for k in (4, 5, 2, 1) if width % (k * HD) == 0)


def fused_call(mesh, *args):
    args = list(args)
    for at in (4, 5):
        args[at] = args[at].transpose(1, 0, 2)
    window, _, _, _, level_table, action_table, w_qkv, w_out, cache_keys, cache_values, _ = args
    F, N = mesh.shape["frame"], mesh.shape["fsdp"]
    T, D = window.shape[1:]
    R, C = cache_keys.shape
    FT = N * T
    Z = N // PAIR
    n = pieces_of(D)
    Dc = D // n
    bf, f32 = jnp.bfloat16, jnp.float32
    vmem = pl.BlockSpec(memory_space=pltpu.VMEM)
    smem = pl.BlockSpec(memory_space=pltpu.SMEM)
    anys = pl.BlockSpec(memory_space=pl.ANY)
    dma = pltpu.SemaphoreType.DMA
    scratch = [
        pltpu.VMEM(level_table.shape, f32),
        pltpu.VMEM(action_table.shape, f32),
        pltpu.VMEM(w_qkv.shape, bf),
        pltpu.VMEM(w_out.shape, bf),
        pltpu.VMEM((2, R, C), bf),
        pltpu.VMEM((F, R, HD), bf),
        pltpu.VMEM((F, R, HD), bf),
        pltpu.VMEM((n, N, T, Dc), bf),
        pltpu.VMEM((T, D), bf),
        pltpu.VMEM((1, D), f32),
        pltpu.VMEM((1, D), f32),
        pltpu.VMEM((3, FT, C), f32),
        pltpu.VMEM((F, 3, FT, HD), bf),
        pltpu.VMEM((F, 3, FT, HD), bf),
        pltpu.VMEM((2, FT, C), bf),
        pltpu.VMEM((2, FT, C), bf),
        pltpu.VMEM((F, FT, HD), bf),
        pltpu.VMEM((FT, C), bf),
        pltpu.VMEM((N, T, Dc), f32),
        pltpu.VMEM((n, Z, T, Dc), f32),
        pltpu.VMEM((n, Z, T, Dc), bf),
        pltpu.VMEM((n, Z, T, Dc), bf),
        pltpu.VMEM((n, Z, T, Dc), bf),
        pltpu.VMEM((n, Z, T, Dc), bf),
        pltpu.VMEM((n, Z, T, Dc), bf),
        pltpu.VMEM((n, Z, T, Dc), bf),
        pltpu.VMEM((n, T, Dc), bf),
        pltpu.VMEM((n, T, Dc), bf),
        pltpu.VMEM((2, R, C), bf),
        dma((9,)),
        dma((n,)),
        dma((n, Z, 3)),
        dma((n, N)),
        dma((2, F)),
        dma((2, F)),
        dma((2,)),
        dma((2,)),
        dma((F,)),
        dma((F,)),
        dma((F,)),
        dma((F,)),
        dma((F,)),
        dma((1,)),
        dma((n,)),
        dma((n,)),
        dma((n, Z)),
        dma((n, Z)),
        dma((n, Z)),
        dma((n, Z)),
        dma((n, F)),
        dma((n,)),
    ]
    results = pl.pallas_call(
        functools.partial(fused, F, N, n),
        out_shape=(
            jax.ShapeDtypeStruct(window.shape, bf),
            jax.ShapeDtypeStruct(window.shape[1:], bf),
            jax.ShapeDtypeStruct(cache_keys.shape, bf),
            jax.ShapeDtypeStruct(cache_values.shape, bf),
        ),
        in_specs=[vmem, smem, smem, smem, anys, anys, anys, anys, anys, anys, vmem],
        out_specs=(vmem, vmem, anys, anys),
        scratch_shapes=scratch,
        compiler_params=pltpu.CompilerParams(
            collective_id=0, has_side_effects=True, vmem_limit_bytes=VMEM_BYTES
        ),
    )(*args)
    return pl.pallas_call(
        hand_out,
        out_shape=tuple(jax.ShapeDtypeStruct(r.shape, r.dtype) for r in results),
        in_specs=[anys] * 4,
        out_specs=(anys,) * 4,
        scratch_shapes=[dma((4,))],
    )(*results)


def dispatch(mesh, *args):
    window, w_qkv, cache_keys = args[0], args[6], args[8]
    F, N = mesh.shape["frame"], mesh.shape["fsdp"]
    heads = w_qkv.shape[2] // HD
    suits = (
        tuple(mesh.axis_names) == ("frame", "fsdp")
        and F > 1
        and heads == F
        and window.shape[0] == 1
        and N % PAIR == 0
        and window.shape[1] % 16 == 0
        and cache_keys.shape[0] % 16 == 0
    )
    if suits:
        return fused_call(mesh, *args)
    return on_device(*args)


def solution(mesh):
    in_specs = (
        P("frame", "fsdp", None),
        P("frame"),
        P("frame"),
        P(),
        P(),
        P(),
        P(None, None, "fsdp"),
        P("fsdp", None),
        P("frame", "fsdp"),
        P("frame", "fsdp"),
        P("fsdp", None),
    )
    out_specs = (P("frame", "fsdp", None), P("fsdp", None), P("frame", "fsdp"), P("frame", "fsdp"))
    return jax.shard_map(
        functools.partial(dispatch, mesh), mesh=mesh, in_specs=in_specs, out_specs=out_specs, check_vma=False
    )
```
